512 devices in a mesh: dp: 128 (over x, z, core), split: 4 (over y).
Axes of the slice: x: 4, y: 4, z: 16, core: 2. Of those that a mesh axis runs over, the one named last changes fastest.
Arguments:
- embeddings: bfloat16 [131072, 768], P(('dp', 'split')), may hold values from -100 to 100
- cluster_ids: int32 [131072, 1], P(('dp', 'split')), may hold values from 0 to 255; in each aligned block of 256 rows (0 to 255, 256 to 511, ...) at most 4 rows name the same one
- order_ranks: int32 [131072], P(('dp', 'split')), may hold values from 0 to 131071, each once
Outputs:
- nearest: float32 [131072], P(('dp', 'split'))
The draws below stay inside these ranges and needn't reach their ends.
Inputs may be any that keep to these rules, and one draw needn't show every extreme that they name: `cluster_ids`: among the 256 rows of one device (aligned blocks in order) no cluster is named more than 4 times, a bound that some block reaches; every cluster is named by some row. `order_ranks`: each rank appears once.
All inputs are finite; a program needn't handle non-finite values.
Results may differ from the reference program's by a relative error of at most 0.00056.
Values may be sent and summed in bfloat16 or wider, within the bound.
A program may use at most 64 MiB of HBM per device.

```python
import math
import jax
import jax.numpy as jnp
import numpy as np
from jax import lax

D = 768
CLUSTERS = 256
MOST = 4
ROWS_DEV = 256
ROWS = 131072
N_DP = 128
N_SPLIT = 4


def draw_embeddings(key, part):
    key = jax.random.fold_in(key, 7)
    common_key, weight_key, jitter_key = jax.random.split(key, 3)
    common = jax.random.truncated_normal(common_key, -4.0, 4.0, (D,), jnp.float32)
    weight = jax.random.uniform(weight_key, (ROWS, 1), jnp.float32, 0.3, 1.2)
    jitter = jax.random.truncated_normal(jitter_key, -4.0, 4.0, (ROWS, D), jnp.float32)
    return (weight * common[None, :] + jitter).astype(jnp.bfloat16)


def assign_block(stream_key, own, number, rows, count, top, limit, lean):
    sequence = jax.random.permutation(stream_key, count)
    heavy_load, usual = load_shares(count, rows * top, limit, lean, True), load_shares(count, rows * top, limit, lean, False)
    places = jnp.arange(count)

    def named(lengths, turn):
        used = int((lengths > 0).sum())
        fixed = max(1, used // 4)
        moved = fixed + (places - fixed + turn * (used - fixed)) % max(1, count - fixed)
        return jnp.zeros((count,), jnp.int32).at[sequence[jnp.where(places < fixed, places, moved)]].set(jnp.asarray(lengths, jnp.int32))

    lengths = jnp.where(number % 4 == 0, named(heavy_load, number // 4), named(usual, number - number // 4 - 1))
    mixed = jax.random.permutation(jax.random.fold_in(own, 3), count)
    giver, taker = mixed[0:count // 2 * 2:2], mixed[1:count // 2 * 2:2]
    room = jnp.minimum(lengths[giver] - 1, limit - lengths[taker]) // 2
    room = jnp.where((giver == sequence[0]) | (taker == sequence[0]) | (lengths[taker] == 0), 0, jnp.maximum(room, 0))
    moved = jax.random.randint(jax.random.fold_in(own, 4), (count // 2,), 0, 1 << 20) % (room + 1)
    lengths = lengths.at[giver].add(-moved).at[taker].add(moved)
    labels = jnp.searchsorted(jnp.cumsum(lengths), jnp.arange(rows * top), side="right").astype(jnp.int32)
    grid = labels.reshape(top, rows).T
    grid = grid[jax.random.permutation(jax.random.fold_in(own, 1), rows)]
    turn = jax.random.randint(jax.random.fold_in(own, 2), (rows, 1), 0, top)
    return jnp.take_along_axis(grid, (jnp.arange(top)[None, :] + turn) % top, axis=1)


def load_shares(count, total, reach, skew, full):
    weights = [(1 << 20) // math.isqrt(rank ** skew) + 1 for rank in range(1, count + 1)]
    largest = reach if full else min(reach, max(-(-total // count), total * weights[0] // sum(weights)))
    least = 1 if total - largest >= count - 1 else 0
    given, surplus = [largest] + [least] * (count - 1), total - largest - least * (count - 1)
    while surplus > 0:
        movable = [i for i in range(1, count) if given[i] < largest] or [i for i in range(1, count) if given[i] < reach]
        mass, remaining = sum([weights[i] for i in movable]), surplus
        for i in movable:
            extra = min(reach - given[i], max(1, remaining * weights[i] // mass), surplus)
            given[i] = given[i] + extra
            surplus = surplus - extra
    return np.array(given)


def setup_inputs(seed: int = 0) -> dict:
    key_of = jax.random.split(jax.random.key(seed), 4)
    embeddings = draw_embeddings(jax.random.fold_in(key_of[3], 71), 0)
    cluster_ids_keys = jax.random.split(jax.random.fold_in(key_of[1], 1), ROWS // ROWS_DEV)
    cluster_ids_turns = jax.random.permutation(jax.random.fold_in(key_of[1], 3), ROWS // ROWS_DEV)
    cluster_ids = jax.vmap(lambda own, number: assign_block(jax.random.fold_in(key_of[1], 2), own, number, ROWS_DEV, CLUSTERS, 1, MOST, 2))(cluster_ids_keys, cluster_ids_turns).reshape((ROWS, 1))
    order_ranks = jax.random.permutation(key_of[2], ROWS).astype(jnp.int32)
    return dict(embeddings=embeddings, cluster_ids=cluster_ids, order_ranks=order_ranks)


def unit_rows(embeddings):
    values = embeddings.astype(jnp.float32)
    factor = lax.rsqrt(lax.optimization_barrier(jnp.mean(values * values, axis=-1, keepdims=True)) + 1e-06) * (1.0 / math.sqrt(values.shape[-1]))
    return (values * factor).astype(jnp.bfloat16)

def reference(embeddings, cluster_ids, order_ranks):
    unit = unit_rows(embeddings)
    cluster = cluster_ids[:, 0]
    ordering = jnp.argsort(cluster, stable=True).astype(jnp.int32)
    sorted_unit = unit[ordering]
    sorted_cluster = cluster[ordering]
    sorted_rank = order_ranks[ordering]
    counts = jnp.zeros((CLUSTERS,), jnp.int32).at[cluster].add(1)
    starts = (jnp.cumsum(counts) - counts).astype(jnp.int32)
    block = min(512, ROWS)
    largest = MOST * N_DP * N_SPLIT
    window = min(ROWS, block + 2 * largest)

    def one_block(number):
        first = (number * block).astype(jnp.int32)
        queries = lax.dynamic_slice_in_dim(sorted_unit, first, block, 0)
        query_cluster = lax.dynamic_slice_in_dim(sorted_cluster, first, block, 0)
        query_rank = lax.dynamic_slice_in_dim(sorted_rank, first, block, 0)
        begin = jnp.clip(starts[sorted_cluster[first]], 0, ROWS - window).astype(jnp.int32)
        key_rows = lax.dynamic_slice_in_dim(sorted_unit, begin, window, 0)
        key_cluster = lax.dynamic_slice_in_dim(sorted_cluster, begin, window, 0)
        key_rank = lax.dynamic_slice_in_dim(sorted_rank, begin, window, 0)
        scores = jnp.dot(queries.astype(jnp.float32), key_rows.astype(jnp.float32).T, preferred_element_type=jnp.float32)
        allowed = (query_cluster[:, None] == key_cluster[None, :]) & (key_rank[None, :] < query_rank[:, None])
        return lax.optimization_barrier(jnp.max(jnp.where(allowed, scores, -1.0), axis=1))
    blocks = lax.map(one_block, jnp.arange(ROWS // block, dtype=jnp.int32))
    return jnp.zeros((ROWS,), jnp.float32).at[ordering].set(blocks.reshape(ROWS))
```

```python
from functools import partial
import math

import jax
import jax.numpy as jnp
from jax import lax
from jax.experimental import pallas as pl
from jax.experimental.pallas import tpu as pltpu
from jax.sharding import PartitionSpec as P

CLUSTERS = 256
MOST = 4
MESH = pl.DeviceIdType.MESH

NX, NY, NZ = 4, 4, 16
ROWS = 256
WIDTH = 768
CAP = 32
GROUP = 4
GROUPS = NZ // GROUP
SLOTS = 16
ZG = CAP * GROUP
XG = SLOTS * NX * NY
BIG = 1 << 22
FAR = float(1 << 20)

STEPS = [0]
for _d in range(1, 8):
    STEPS += [_d, NZ - _d]
STEPS.append(8)


def unit_rows(embeddings):
    values = embeddings.astype(jnp.float32)
    factor = lax.rsqrt(jnp.mean(values * values, axis=-1, keepdims=True) + 1e-06) * (
        1.0 / math.sqrt(values.shape[-1])
    )
    return (values * factor).astype(jnp.bfloat16)


def iota(shape, axis):
    return lax.broadcasted_iota(jnp.int32, shape, axis)


def one_hot(row, count):
    return jnp.where(iota((count, row.shape[1]), 0) == row, 1.0, 0.0)


def places(member):
    n = member.shape[1]
    before = jnp.where(iota((n, n), 0) < iota((n, n), 1), 1.0, 0.0).astype(jnp.bfloat16)
    counts = jnp.dot(member.astype(jnp.bfloat16), before, preferred_element_type=jnp.float32)
    return jnp.sum(member * counts, axis=0, keepdims=True).astype(jnp.int32)


def three_rows(a, b, c):
    sub = iota((8, a.shape[1]), 0)
    rows = jnp.where(sub == 0, a, jnp.where(sub == 1, b, jnp.where(sub == 2, c, 0.0)))
    return rows.astype(jnp.bfloat16)


def place_codes(codes, hot):
    parts = three_rows(
        (codes >> 16).astype(jnp.float32),
        ((codes >> 8) & 255).astype(jnp.float32),
        (codes & 255).astype(jnp.float32),
    )
    moved = lax.dot_general(parts, hot, (((1,), (1,)), ((), ())), preferred_element_type=jnp.float32)
    return (moved[0:1] * 65536.0 + moved[1:2] * 256.0 + moved[2:3]).astype(jnp.int32)


def fetch_values(values, hot):
    high = values.astype(jnp.bfloat16).astype(jnp.float32)
    rest = values - high
    middle = rest.astype(jnp.bfloat16).astype(jnp.float32)
    parts = three_rows(high, middle, rest - middle)
    moved = jnp.dot(parts, hot, preferred_element_type=jnp.float32)
    return (moved[0:1] + moved[1:2]) + moved[2:3]


def kernel(
    emb, cluster, rank, out, flag,
    hot1, hot2, zsend, zrecv, xysend, own, other, key_rank,
    zmeta_out, zmeta_in, xymeta_out, xymeta_in, own_meta, other_meta,
    best_out, xyback, zback_out, zback,
    zmeta_sem, zrow_send, zrow_recv, xymeta_sem, xyrow_send, xyrow_recv,
    cmeta_sem, crow_send, crow_recv, xyback_sem, zback_sem,
):
    dp, y = lax.axis_index("dp"), lax.axis_index("split")
    x, z, core = dp // (2 * NZ), (dp // 2) % NZ, dp % 2

    def along_z(step):
        return ((x * NZ + (z + step + NZ) % NZ) * 2 + core, y)

    def in_plane(e, sign):
        there_x = (x + sign * (e // NY) + NX) % NX
        there_y = (y + sign * (e % NY) + NY) % NY
        return ((there_x * NZ + z) * 2 + core, there_y)

    partner = (dp + 1 - 2 * core, y)

    barrier = pltpu.get_barrier_semaphore()
    for i in range(1, NZ):
        pl.semaphore_signal(barrier, inc=1, device_id=along_z(STEPS[i]), device_id_type=MESH)
    for e in range(1, NX * NY):
        pl.semaphore_signal(barrier, inc=1, device_id=in_plane(e, 1), device_id_type=MESH)
    pl.semaphore_signal(barrier, inc=1, device_id=partner, device_id_type=MESH)

    def send(src, dst, send_sem, recv_sem, device):
        pltpu.make_async_remote_copy(
            src_ref=src, dst_ref=dst, send_sem=send_sem, recv_sem=recv_sem, device_id=device, device_id_type=MESH
        ).start()

    def wait(ref, sem):
        pltpu.make_async_copy(ref, ref, sem).wait()

    ids = cluster[...]
    away = ((ids >> 4) - z) & (NZ - 1)
    step = jnp.where(away == 0, 0, jnp.where(away <= 8, 2 * away - 1, 2 * (NZ - away)))
    place = places(one_hot(step, NZ))
    slot = jnp.where(place < CAP, step * CAP + place, -1)
    most = jnp.max(place.astype(jnp.float32), axis=1, keepdims=True)
    codes = (ids & 15) * 131072 + rank[...] + 1
    for g in range(GROUPS):
        hot = one_hot(slot - g * ZG, ZG).astype(jnp.bfloat16)
        hot1[g * ZG : (g + 1) * ZG, :] = hot
        zmeta_out[g] = jnp.where(most >= CAP, BIG, place_codes(codes, hot))
    zmeta_in[0] = zmeta_out[0]

    unit = unit_rows(emb[...])
    pl.semaphore_wait(barrier, NZ - 1 + NX * NY - 1 + 1)
    for i in range(1, NZ):
        send(zmeta_out.at[i // GROUP], zmeta_in.at[i], zmeta_sem.at[0], zmeta_sem.at[1], along_z(STEPS[i]))
    for g in range(GROUPS):
        rows = jnp.dot(hot1[g * ZG : (g + 1) * ZG, :], unit, preferred_element_type=jnp.float32).astype(jnp.bfloat16)
        zsend[g * ZG : (g + 1) * ZG, :] = rows
        if g == 0:
            zrecv[0:CAP, :] = rows[0:CAP]
        for i in range(max(1, g * GROUP), (g + 1) * GROUP):
            at = pl.ds(i * CAP, CAP)
            send(zsend.at[at], zrecv.at[at], zrow_send.at[0], zrow_recv.at[g], along_z(STEPS[i]))

    wait(zmeta_in.at[pl.ds(1, NZ - 1)], zmeta_sem.at[1])
    lane = iota((1, 128), 1)
    sub = iota((8, 128), 0)
    over = jnp.zeros((1, 1), jnp.float32)
    meta = [jnp.zeros((8, 128), jnp.int32), jnp.zeros((8, 128), jnp.int32)]
    for g in range(GROUPS):
        codes = zmeta_in[g * GROUP]
        for q in range(1, GROUP):
            codes = jnp.where(lane // CAP == q, zmeta_in[g * GROUP + q], codes)
        over = jnp.maximum(over, jnp.max(codes.astype(jnp.float32), axis=1, keepdims=True))
        filled = (codes > 0) & (codes < BIG)
        value = codes - 1
        local = value >> 17
        e = (((local >> 2) - x) & 3) * NY + (((local & 3) - y) & 3)
        e = jnp.where(filled, e, NX * NY)
        slot2 = jnp.where(filled, e * SLOTS + places(one_hot(e, NX * NY)), -1)
        hot = one_hot(slot2, XG).astype(jnp.bfloat16)
        hot2[g * XG : (g + 1) * XG, :] = hot
        ranks = place_codes(jnp.where(filled, (value & 131071) + 1, 0), hot)
        for h in range(2):
            meta[h] = jnp.where(sub == g, ranks[:, h * 128 : (h + 1) * 128], meta[h])
    for h in range(2):
        xymeta_out[h] = jnp.where(over >= BIG, BIG, meta[h])
    xymeta_in[0] = xymeta_out[0]
    for e in range(1, NX * NY):
        send(xymeta_out.at[e // 8], xymeta_in.at[e], xymeta_sem.at[0], xymeta_sem.at[1], in_plane(e, 1))
    wait(xymeta_in.at[pl.ds(1, NX * NY - 1)], xymeta_sem.at[1])
    lane8 = iota((8, 128), 1)
    for h in range(2):
        merged = xymeta_in[h * 8]
        for e in range(1, 8):
            merged = jnp.where(lane8 // SLOTS == e, xymeta_in[h * 8 + e], merged)
        own_meta[h] = merged
    send(own_meta, other_meta, cmeta_sem.at[0], cmeta_sem.at[1], partner)
    wait(other_meta, cmeta_sem.at[1])
    top = jnp.zeros((8, 128), jnp.float32)
    query_rank = []
    for which, ref in enumerate((own_meta, other_meta)):
        for h in range(2):
            tile = ref[h]
            top = jnp.maximum(top, tile.astype(jnp.float32))
            for g in range(GROUPS):
                row = tile[g : g + 1].astype(jnp.float32)
                key = jnp.where(row > 0.0, row, FAR)
                at = which * GROUPS * XG + g * XG + h * 128
                key_rank[at : at + 128, :] = jnp.transpose(jnp.broadcast_to(key, (128, 128)))
    flag[...] = jnp.where(jnp.max(top, axis=(0, 1), keepdims=True) >= BIG, 1, 0) + jnp.zeros((8, 128), jnp.int32)
    for g in range(GROUPS):
        query_rank.append(
            jnp.concatenate([own_meta[0][g : g + 1], own_meta[1][g : g + 1]], axis=1).astype(jnp.float32)
        )
    best = [jnp.full((1, XG), -1.0, jnp.float32) for _ in range(GROUPS)]

    def score(which, first, last, g0, g1):
        ref = (own, other)[which]
        scores = lax.dot_general(
            ref[first * XG : last * XG, :],
            own[g0 * XG : g1 * XG, :],
            (((1,), (1,)), ((), ())),
            preferred_element_type=jnp.float32,
        )
        base = which * GROUPS * XG
        ranks = key_rank[base + first * XG : base + last * XG, :]
        for g in range(g0, g1):
            for h in range(2):
                at = (g - g0) * XG + h * 128
                earlier = ranks < query_rank[g][:, h * 128 : (h + 1) * 128]
                part = jnp.max(jnp.where(earlier, scores[:, at : at + 128], -1.0), axis=0, keepdims=True)
                halves[g][h] = jnp.maximum(halves[g][h], part)

    halves = [[row[:, 0:128], row[:, 128:256]] for row in best]

    def score_group(which, g):
        score(which, 0, g + 1, g, g + 1)
        if g:
            score(which, g, g + 1, 0, g)

    def group_in_plane(g):
        first = max(1, g * GROUP)
        wait(zrecv.at[pl.ds(first * CAP, ((g + 1) * GROUP - first) * CAP)], zrow_recv.at[g])
        rows = jnp.dot(
            hot2[g * XG : (g + 1) * XG, :], zrecv[g * ZG : (g + 1) * ZG, :], preferred_element_type=jnp.float32
        ).astype(jnp.bfloat16)
        xysend[g * XG : (g + 1) * XG, :] = rows
        own[g * XG : g * XG + SLOTS, :] = rows[0:SLOTS]
        for e in range(1, NX * NY):
            at = pl.ds(g * XG + e * SLOTS, SLOTS)
            send(xysend.at[at], own.at[at], xyrow_send.at[0], xyrow_recv.at[g], in_plane(e, 1))

    def group_to_partner(g):
        wait(own.at[pl.ds(g * XG + SLOTS, XG - SLOTS)], xyrow_recv.at[g])
        at = pl.ds(g * XG, XG)
        send(own.at[at], other.at[at], crow_send.at[0], crow_recv.at[g], partner)

    def group_from_partner(g):
        wait(other.at[pl.ds(g * XG, XG)], crow_recv.at[g])

    for g in range(GROUPS):
        group_in_plane(g)
        if g >= 1:
            group_to_partner(g - 1)
        if g >= 2:
            group_from_partner(g - 2)
            for which in range(2):
                score_group(which, g - 2)
    group_from_partner(GROUPS - 2)
    for which in range(2):
        score_group(which, GROUPS - 2)
    group_to_partner(GROUPS - 1)
    score_group(0, GROUPS - 1)
    group_from_partner(GROUPS - 1)
    score_group(1, GROUPS - 1)

    for h in range(2):
        tile = jnp.zeros((8, 128), jnp.float32)
        for g in range(GROUPS):
            tile = jnp.where(sub == g, halves[g][h], tile)
        best_out[h] = tile
    xyback[0] = best_out[0]
    for e in range(1, NX * NY):
        send(best_out.at[e // 8], xyback.at[e], xyback_sem.at[0], xyback_sem.at[1], in_plane(e, -1))
    wait(xyback.at[pl.ds(1, NX * NY - 1)], xyback_sem.at[1])
    merged = []
    for h in range(2):
        tile = xyback[h * 8]
        for e in range(1, 8):
            tile = jnp.where(lane8 // SLOTS == e, xyback[h * 8 + e], tile)
        merged.append(tile)
    for g in range(GROUPS):
        row = jnp.concatenate([merged[0][g : g + 1], merged[1][g : g + 1]], axis=1)
        zback_out[g] = fetch_values(row, hot2[g * XG : (g + 1) * XG, :])
    zback[0] = zback_out[0]
    for i in range(1, NZ):
        send(zback_out.at[i // GROUP], zback.at[i], zback_sem.at[0], zback_sem.at[1], along_z(-STEPS[i]))
    wait(zback.at[pl.ds(1, NZ - 1)], zback_sem.at[1])
    parts = []
    for g in range(GROUPS):
        row = zback[g * GROUP]
        for q in range(1, GROUP):
            row = jnp.where(lane // CAP == q, zback[g * GROUP + q], row)
        parts.append(row)
    out[...] = fetch_values(jnp.concatenate(parts, axis=1), hot1[...])

    wait(zmeta_in.at[pl.ds(1, NZ - 1)], zmeta_sem.at[0])
    wait(zsend.at[pl.ds(CAP, (NZ - 1) * CAP)], zrow_send.at[0])
    wait(xymeta_in.at[pl.ds(1, NX * NY - 1)], xymeta_sem.at[0])
    for g in range(GROUPS):
        wait(own.at[pl.ds(g * XG + SLOTS, XG - SLOTS)], xyrow_send.at[0])
    wait(own_meta, cmeta_sem.at[0])
    wait(own, crow_send.at[0])
    wait(xyback.at[pl.ds(1, NX * NY - 1)], xyback_sem.at[0])
    wait(zback.at[pl.ds(1, NZ - 1)], zback_sem.at[0])


def fast(embeddings, cluster_ids, order_ranks):
    vmem = pl.BlockSpec(memory_space=pltpu.VMEM)
    bf16, f32, i32 = jnp.bfloat16, jnp.float32, jnp.int32
    pair = pltpu.SemaphoreType.DMA((2,))
    one = pltpu.SemaphoreType.DMA((1,))
    each = pltpu.SemaphoreType.DMA((GROUPS,))
    return pl.pallas_call(
        kernel,
        out_shape=(jax.ShapeDtypeStruct((1, ROWS), f32), jax.ShapeDtypeStruct((8, 128), i32)),
        in_specs=[vmem] * 3,
        out_specs=(vmem, vmem),
        scratch_shapes=[
            pltpu.VMEM((GROUPS * ZG, ROWS), bf16),
            pltpu.VMEM((GROUPS * XG, ZG), bf16),
            pltpu.VMEM((GROUPS * ZG, WIDTH), bf16),
            pltpu.VMEM((GROUPS * ZG, WIDTH), bf16),
            pltpu.VMEM((GROUPS * XG, WIDTH), bf16),
            pltpu.VMEM((GROUPS * XG, WIDTH), bf16),
            pltpu.VMEM((GROUPS * XG, WIDTH), bf16),
            pltpu.VMEM((2 * GROUPS * XG, 128), f32),
            pltpu.VMEM((GROUPS, 1, 128), i32),
            pltpu.VMEM((NZ, 1, 128), i32),
            pltpu.VMEM((2, 8, 128), i32),
            pltpu.VMEM((NX * NY, 8, 128), i32),
            pltpu.VMEM((2, 8, 128), i32),
            pltpu.VMEM((2, 8, 128), i32),
            pltpu.VMEM((2, 8, 128), f32),
            pltpu.VMEM((NX * NY, 8, 128), f32),
            pltpu.VMEM((GROUPS, 1, 128), f32),
            pltpu.VMEM((NZ, 1, 128), f32),
            pair, one, each, pair, one, each, pair, one, each, pair, pair,
        ],
        compiler_params=pltpu.CompilerParams(
            collective_id=0, has_side_effects=True, vmem_limit_bytes=40 * 1024 * 1024
        ),
    )(embeddings, cluster_ids.reshape(1, ROWS), order_ranks.reshape(1, ROWS))


def pair_tile(queries, query_cluster, query_rank, key_rows, key_cluster, key_rank):
    scores = lax.dot_general(queries, key_rows, (((1,), (1,)), ((), ())), preferred_element_type=jnp.float32)
    same = (query_cluster[:, None] == key_cluster[None, :]) & (query_cluster[:, None] >= 0)
    row_mask = same & (key_rank[None, :] < query_rank[:, None])
    return jnp.max(jnp.where(row_mask, scores, -1.0), axis=1)


def padded(embeddings, cluster_ids, order_ranks):
    owner_count = lax.axis_size("dp")
    per_owner = CLUSTERS // owner_count
    capacity = per_owner * MOST
    slot_total = owner_count * capacity
    unit = unit_rows(embeddings)
    cluster = cluster_ids[:, 0]
    position = jnp.arange(cluster.shape[0], dtype=jnp.int32)
    earlier = (cluster[:, None] == cluster[None, :]) & (position[None, :] < position[:, None])
    place = jnp.sum(earlier.astype(jnp.int32), axis=1)
    target = cluster // per_owner * capacity + cluster % per_owner * MOST + place
    send_rows = jnp.zeros((slot_total, embeddings.shape[1]), jnp.bfloat16).at[target].set(unit)
    send_cluster = jnp.full((slot_total,), -1, jnp.int32).at[target].set(cluster)
    send_rank = jnp.zeros((slot_total,), jnp.int32).at[target].set(order_ranks)
    slots = [
        lax.all_to_all(a, "dp", split_axis=0, concat_axis=0, tiled=True) for a in (send_rows, send_cluster, send_rank)
    ]
    pieces = [lax.all_gather(a, "split", axis=0, tiled=True) for a in slots]
    tile = 512
    parts = []
    for begin in range(0, slot_total, tile):
        mine = [a[begin : begin + tile] for a in slots]
        best = jnp.full((tile,), -1.0, jnp.float32)
        for key in range(0, pieces[0].shape[0], tile):
            best = jnp.maximum(best, pair_tile(*mine, *[a[key : key + tile] for a in pieces]))
        parts.append(best)
    returned = lax.all_to_all(jnp.concatenate(parts), "dp", split_axis=0, concat_axis=0, tiled=True)
    return returned[target]


def shards(embeddings, cluster_ids, order_ranks):
    nearest, flag = fast(embeddings, cluster_ids, order_ranks)
    return lax.cond(
        flag[0, 0] > 0,
        lambda: padded(embeddings, cluster_ids, order_ranks),
        lambda: nearest.reshape(ROWS),
    )


def solution(mesh):
    in_specs = (P(("dp", "split"), None), P(("dp", "split"), None), P(("dp", "split")))
    out_specs = P(("dp", "split"))
    return jax.shard_map(shards, mesh=mesh, in_specs=in_specs, out_specs=out_specs, check_vma=False)
```

```python
from functools import partial
import math

import jax
import jax.numpy as jnp
from jax import lax
from jax.experimental import pallas as pl
from jax.experimental.pallas import tpu as pltpu
from jax.sharding import PartitionSpec as P

MESH = pl.DeviceIdType.MESH

NX, NY, NZ = 4, 4, 16
ROWS = 256
WIDTH = 768
CAP = 32
FULL = 64
GROUP = 4
GROUPS = NZ // GROUP
SLOTS = 16
XG = SLOTS * NX * NY
BIG = 1 << 22
FAR = float(1 << 20)

STEPS = [0]
for _d in range(1, 8):
    STEPS += [_d, NZ - _d]
STEPS.append(8)


def unit_rows(embeddings):
    values = embeddings.astype(jnp.float32)
    factor = lax.rsqrt(jnp.mean(values * values, axis=-1, keepdims=True) + 1e-06) * (
        1.0 / math.sqrt(values.shape[-1])
    )
    return (values * factor).astype(jnp.bfloat16)


def iota(shape, axis):
    return lax.broadcasted_iota(jnp.int32, shape, axis)


def one_hot(row, count):
    return jnp.where(iota((count, row.shape[1]), 0) == row, 1.0, 0.0)


def places(member):
    n = member.shape[1]
    before = jnp.where(iota((n, n), 0) < iota((n, n), 1), 1.0, 0.0).astype(jnp.bfloat16)
    counts = jnp.dot(member.astype(jnp.bfloat16), before, preferred_element_type=jnp.float32)
    return jnp.sum(member * counts, axis=0, keepdims=True).astype(jnp.int32)


def three_rows(a, b, c):
    sub = iota((8, a.shape[1]), 0)
    rows = jnp.where(sub == 0, a, jnp.where(sub == 1, b, jnp.where(sub == 2, c, 0.0)))
    return rows.astype(jnp.bfloat16)


def place_codes(codes, hot):
    parts = three_rows(
        (codes >> 16).astype(jnp.float32),
        ((codes >> 8) & 255).astype(jnp.float32),
        (codes & 255).astype(jnp.float32),
    )
    moved = lax.dot_general(parts, hot, (((1,), (1,)), ((), ())), preferred_element_type=jnp.float32)
    return (moved[0:1] * 65536.0 + moved[1:2] * 256.0 + moved[2:3]).astype(jnp.int32)


def fetch_values(values, hot):
    high = values.astype(jnp.bfloat16).astype(jnp.float32)
    rest = values - high
    middle = rest.astype(jnp.bfloat16).astype(jnp.float32)
    parts = three_rows(high, middle, rest - middle)
    moved = jnp.dot(parts, hot, preferred_element_type=jnp.float32)
    return (moved[0:1] + moved[1:2]) + moved[2:3]


def kernel(
    cap,
    emb, cluster, rank, out, flag,
    hot1, hot2, zsend, zrecv, xysend, own, other, key_rank,
    zmeta_out, zmeta_in, xymeta_out, xymeta_in, own_meta, other_meta,
    best_out, xyback, zback_out, zback,
    zmeta_sem, zrow_send, zrow_recv, xymeta_sem, xyrow_send, xyrow_recv,
    cmeta_sem, crow_send, crow_recv, xyback_sem, zback_sem,
):
    zg = cap * GROUP
    per = 128 // cap
    tiles = zg // 128
    dp, y = lax.axis_index("dp"), lax.axis_index("split")
    x, z, core = dp // (2 * NZ), (dp // 2) % NZ, dp % 2

    def along_z(step):
        return ((x * NZ + (z + step + NZ) % NZ) * 2 + core, y)

    def in_plane(e, sign):
        there_x = (x + sign * (e // NY) + NX) % NX
        there_y = (y + sign * (e % NY) + NY) % NY
        return ((there_x * NZ + z) * 2 + core, there_y)

    partner = (dp + 1 - 2 * core, y)

    barrier = pltpu.get_barrier_semaphore()
    for i in range(1, NZ):
        pl.semaphore_signal(barrier, inc=1, device_id=along_z(STEPS[i]), device_id_type=MESH)
    for e in range(1, NX * NY):
        pl.semaphore_signal(barrier, inc=1, device_id=in_plane(e, 1), device_id_type=MESH)
    pl.semaphore_signal(barrier, inc=1, device_id=partner, device_id_type=MESH)

    def send(src, dst, send_sem, recv_sem, device):
        pltpu.make_async_remote_copy(
            src_ref=src, dst_ref=dst, send_sem=send_sem, recv_sem=recv_sem, device_id=device, device_id_type=MESH
        ).start()

    def wait(ref, sem):
        pltpu.make_async_copy(ref, ref, sem).wait()

    ids = cluster[...]
    away = ((ids >> 4) - z) & (NZ - 1)
    step = jnp.where(away == 0, 0, jnp.where(away <= 8, 2 * away - 1, 2 * (NZ - away)))
    place = places(one_hot(step, NZ))
    slot = jnp.where(place < cap, step * cap + place, -1)
    most = jnp.max(place.astype(jnp.float32), axis=1, keepdims=True)
    codes = (ids & 15) * 131072 + rank[...] + 1
    for g in range(GROUPS):
        hot = one_hot(slot - g * zg, zg).astype(jnp.bfloat16)
        hot1[g * zg : (g + 1) * zg, :] = hot
        placed = jnp.where(most >= cap, BIG, place_codes(codes, hot))
        for t in range(tiles):
            zmeta_out[g * tiles + t] = placed[:, t * 128 : (t + 1) * 128]
    zmeta_in[0] = zmeta_out[0]

    unit = unit_rows(emb[...])
    pl.semaphore_wait(barrier, NZ - 1 + NX * NY - 1 + 1)
    for i in range(1, NZ):
        send(zmeta_out.at[i // per], zmeta_in.at[i], zmeta_sem.at[0], zmeta_sem.at[1], along_z(STEPS[i]))
    for g in range(GROUPS):
        rows = jnp.dot(hot1[g * zg : (g + 1) * zg, :], unit, preferred_element_type=jnp.float32).astype(jnp.bfloat16)
        zsend[g * zg : (g + 1) * zg, :] = rows
        if g == 0:
            zrecv[0:cap, :] = rows[0:cap]
        for i in range(max(1, g * GROUP), (g + 1) * GROUP):
            at = pl.ds(i * cap, cap)
            send(zsend.at[at], zrecv.at[at], zrow_send.at[0], zrow_recv.at[g], along_z(STEPS[i]))

    wait(zmeta_in.at[pl.ds(1, NZ - 1)], zmeta_sem.at[1])
    lane = iota((1, 128), 1)

    def merge(ref, g):
        rows = []
        for first in range(g * GROUP, (g + 1) * GROUP, per):
            row = ref[first]
            for q in range(1, per):
                row = jnp.where(lane // cap == q, ref[first + q], row)
            rows.append(row)
        return rows[0] if tiles == 1 else jnp.concatenate(rows, axis=1)

    sub = iota((8, 128), 0)
    over = jnp.zeros((1, 1), jnp.float32)
    meta = [jnp.zeros((8, 128), jnp.int32), jnp.zeros((8, 128), jnp.int32)]
    for g in range(GROUPS):
        codes = merge(zmeta_in, g)
        over = jnp.maximum(over, jnp.max(codes.astype(jnp.float32), axis=1, keepdims=True))
        filled = (codes > 0) & (codes < BIG)
        value = codes - 1
        local = value >> 17
        e = (((local >> 2) - x) & 3) * NY + (((local & 3) - y) & 3)
        e = jnp.where(filled, e, NX * NY)
        slot2 = jnp.where(filled, e * SLOTS + places(one_hot(e, NX * NY)), -1)
        hot = one_hot(slot2, XG).astype(jnp.bfloat16)
        hot2[g * XG : (g + 1) * XG, :] = hot
        ranks = place_codes(jnp.where(filled, (value & 131071) + 1, 0), hot)
        for h in range(2):
            meta[h] = jnp.where(sub == g, ranks[:, h * 128 : (h + 1) * 128], meta[h])
    for h in range(2):
        xymeta_out[h] = jnp.where(over >= BIG, BIG, meta[h])
    xymeta_in[0] = xymeta_out[0]
    for e in range(1, NX * NY):
        send(xymeta_out.at[e // 8], xymeta_in.at[e], xymeta_sem.at[0], xymeta_sem.at[1], in_plane(e, 1))
    wait(xymeta_in.at[pl.ds(1, NX * NY - 1)], xymeta_sem.at[1])
    lane8 = iota((8, 128), 1)
    for h in range(2):
        merged = xymeta_in[h * 8]
        for e in range(1, 8):
            merged = jnp.where(lane8 // SLOTS == e, xymeta_in[h * 8 + e], merged)
        own_meta[h] = merged
    send(own_meta, other_meta, cmeta_sem.at[0], cmeta_sem.at[1], partner)
    wait(other_meta, cmeta_sem.at[1])
    top = jnp.zeros((8, 128), jnp.float32)
    query_rank = []
    for which, ref in enumerate((own_meta, other_meta)):
        for h in range(2):
            tile = ref[h]
            top = jnp.maximum(top, tile.astype(jnp.float32))
            for g in range(GROUPS):
                row = tile[g : g + 1].astype(jnp.float32)
                key = jnp.where(row > 0.0, row, FAR)
                at = which * GROUPS * XG + g * XG + h * 128
                key_rank[at : at + 128, :] = jnp.transpose(jnp.broadcast_to(key, (128, 128)))
    flag[...] = jnp.where(jnp.max(top, axis=(0, 1), keepdims=True) >= BIG, 1, 0)
    for g in range(GROUPS):
        query_rank.append(
            jnp.concatenate([own_meta[0][g : g + 1], own_meta[1][g : g + 1]], axis=1).astype(jnp.float32)
        )
    best = [jnp.full((1, XG), -1.0, jnp.float32) for _ in range(GROUPS)]

    def score(which, first, last, g0, g1):
        ref = (own, other)[which]
        scores = lax.dot_general(
            ref[first * XG : last * XG, :],
            own[g0 * XG : g1 * XG, :],
            (((1,), (1,)), ((), ())),
            preferred_element_type=jnp.float32,
        )
        base = which * GROUPS * XG
        ranks = key_rank[base + first * XG : base + last * XG, :]
        for g in range(g0, g1):
            for h in range(2):
                at = (g - g0) * XG + h * 128
                earlier = ranks < query_rank[g][:, h * 128 : (h + 1) * 128]
                part = jnp.max(jnp.where(earlier, scores[:, at : at + 128], -1.0), axis=0, keepdims=True)
                halves[g][h] = jnp.maximum(halves[g][h], part)

    halves = [[row[:, 0:128], row[:, 128:256]] for row in best]

    def score_group(which, g):
        score(which, 0, g + 1, g, g + 1)
        if g:
            score(which, g, g + 1, 0, g)

    def group_in_plane(g):
        first = max(1, g * GROUP)
        wait(zrecv.at[pl.ds(first * cap, ((g + 1) * GROUP - first) * cap)], zrow_recv.at[g])
        rows = jnp.dot(
            hot2[g * XG : (g + 1) * XG, :], zrecv[g * zg : (g + 1) * zg, :], preferred_element_type=jnp.float32
        ).astype(jnp.bfloat16)
        xysend[g * XG : (g + 1) * XG, :] = rows
        own[g * XG : g * XG + SLOTS, :] = rows[0:SLOTS]
        for e in range(1, NX * NY):
            at = pl.ds(g * XG + e * SLOTS, SLOTS)
            send(xysend.at[at], own.at[at], xyrow_send.at[0], xyrow_recv.at[g], in_plane(e, 1))

    def group_to_partner(g):
        wait(own.at[pl.ds(g * XG + SLOTS, XG - SLOTS)], xyrow_recv.at[g])
        at = pl.ds(g * XG, XG)
        send(own.at[at], other.at[at], crow_send.at[0], crow_recv.at[g], partner)

    def group_from_partner(g):
        wait(other.at[pl.ds(g * XG, XG)], crow_recv.at[g])

    for g in range(GROUPS):
        group_in_plane(g)
        if g >= 1:
            group_to_partner(g - 1)
        if g >= 2:
            group_from_partner(g - 2)
            for which in range(2):
                score_group(which, g - 2)
    group_from_partner(GROUPS - 2)
    for which in range(2):
        score_group(which, GROUPS - 2)
    group_to_partner(GROUPS - 1)
    score_group(0, GROUPS - 1)
    group_from_partner(GROUPS - 1)
    score_group(1, GROUPS - 1)

    for h in range(2):
        tile = jnp.zeros((8, 128), jnp.float32)
        for g in range(GROUPS):
            tile = jnp.where(sub == g, halves[g][h], tile)
        best_out[h] = tile
    xyback[0] = best_out[0]
    for e in range(1, NX * NY):
        send(best_out.at[e // 8], xyback.at[e], xyback_sem.at[0], xyback_sem.at[1], in_plane(e, -1))
    wait(xyback.at[pl.ds(1, NX * NY - 1)], xyback_sem.at[1])
    merged = []
    for h in range(2):
        tile = xyback[h * 8]
        for e in range(1, 8):
            tile = jnp.where(lane8 // SLOTS == e, xyback[h * 8 + e], tile)
        merged.append(tile)
    for g in range(GROUPS):
        row = jnp.concatenate([merged[0][g : g + 1], merged[1][g : g + 1]], axis=1)
        fetched = fetch_values(row, hot2[g * XG : (g + 1) * XG, :])
        for t in range(tiles):
            zback_out[g * tiles + t] = fetched[:, t * 128 : (t + 1) * 128]
    zback[0] = zback_out[0]
    for i in range(1, NZ):
        send(zback_out.at[i // per], zback.at[i], zback_sem.at[0], zback_sem.at[1], along_z(-STEPS[i]))
    wait(zback.at[pl.ds(1, NZ - 1)], zback_sem.at[1])
    out[...] = fetch_values(jnp.concatenate([merge(zback, g) for g in range(GROUPS)], axis=1), hot1[...])

    wait(zmeta_in.at[pl.ds(1, NZ - 1)], zmeta_sem.at[0])
    wait(zsend.at[pl.ds(cap, (NZ - 1) * cap)], zrow_send.at[0])
    wait(xymeta_in.at[pl.ds(1, NX * NY - 1)], xymeta_sem.at[0])
    for g in range(GROUPS):
        wait(own.at[pl.ds(g * XG + SLOTS, XG - SLOTS)], xyrow_send.at[0])
    wait(own_meta, cmeta_sem.at[0])
    wait(own, crow_send.at[0])
    wait(xyback.at[pl.ds(1, NX * NY - 1)], xyback_sem.at[0])
    wait(zback.at[pl.ds(1, NZ - 1)], zback_sem.at[0])


def exchange(cap, collective_id, embeddings, cluster_ids, order_ranks):
    vmem = pl.BlockSpec(memory_space=pltpu.VMEM)
    bf16, f32, i32 = jnp.bfloat16, jnp.float32, jnp.int32
    pair = pltpu.SemaphoreType.DMA((2,))
    one = pltpu.SemaphoreType.DMA((1,))
    each = pltpu.SemaphoreType.DMA((GROUPS,))
    return pl.pallas_call(
        partial(kernel, cap),
        out_shape=(jax.ShapeDtypeStruct((1, ROWS), f32), jax.ShapeDtypeStruct((1, 1), i32)),
        in_specs=[vmem] * 3,
        out_specs=(vmem, vmem),
        scratch_shapes=[
            pltpu.VMEM((NZ * cap, ROWS), bf16),
            pltpu.VMEM((GROUPS * XG, GROUP * cap), bf16),
            pltpu.VMEM((NZ * cap, WIDTH), bf16),
            pltpu.VMEM((NZ * cap, WIDTH), bf16),
            pltpu.VMEM((GROUPS * XG, WIDTH), bf16),
            pltpu.VMEM((GROUPS * XG, WIDTH), bf16),
            pltpu.VMEM((GROUPS * XG, WIDTH), bf16),
            pltpu.VMEM((2 * GROUPS * XG, 128), f32),
            pltpu.VMEM((NZ * cap // 128, 1, 128), i32),
            pltpu.VMEM((NZ, 1, 128), i32),
            pltpu.VMEM((2, 8, 128), i32),
            pltpu.VMEM((NX * NY, 8, 128), i32),
            pltpu.VMEM((2, 8, 128), i32),
            pltpu.VMEM((2, 8, 128), i32),
            pltpu.VMEM((2, 8, 128), f32),
            pltpu.VMEM((NX * NY, 8, 128), f32),
            pltpu.VMEM((NZ * cap // 128, 1, 128), f32),
            pltpu.VMEM((NZ, 1, 128), f32),
            pair, one, each, pair, one, each, pair, one, each, pair, pair,
        ],
        compiler_params=pltpu.CompilerParams(
            collective_id=collective_id, has_side_effects=True, vmem_limit_bytes=40 * 1024 * 1024
        ),
    )(embeddings, cluster_ids, order_ranks)


def shards(embeddings, cluster_ids, order_ranks):
    args = (embeddings, cluster_ids.reshape(1, ROWS), order_ranks.reshape(1, ROWS))
    nearest, flag = exchange(CAP, 0, *args)
    nearest = lax.cond(flag[0, 0] > 0, lambda: exchange(FULL, 1, *args)[0], lambda: nearest)
    return nearest.reshape(ROWS)


def solution(mesh):
    in_specs = (P(("dp", "split"), None), P(("dp", "split"), None), P(("dp", "split")))
    out_specs = P(("dp", "split"))
    return jax.shard_map(shards, mesh=mesh, in_specs=in_specs, out_specs=out_specs, check_vma=False)
```

```python
from functools import partial
import math

import jax
import jax.numpy as jnp
from jax import lax
from jax.experimental import pallas as pl
from jax.experimental.pallas import tpu as pltpu
from jax.sharding import PartitionSpec as P

MESH = pl.DeviceIdType.MESH

NX, NY, NZ = 4, 4, 16
CHIPS = NX * NY
ROWS = 256
WIDTH = 768
HALF = WIDTH // 2
MOST = 4
CAP = 32
FULL = MOST * CHIPS

STEPS = [0, 8, 4, 12, 7, 9, 1, 15, 6, 10, 2, 14, 3, 13, 5, 11]
COUNTS = [4, 4, 4, 2, 2]
GROUPS = len(COUNTS)
FIRST = [sum(COUNTS[:g]) for g in range(GROUPS)]
GROUP_OF = [g for g in range(GROUPS) for _ in range(COUNTS[g])]
SLOTS = [MOST * n for n in COUNTS]
XG = [CHIPS * n for n in SLOTS]
OFF = [sum(XG[:g]) for g in range(GROUPS)]
TOTAL = sum(XG)
WHOLE = 3
FAR_Z = sorted(range(1, NZ), key=lambda i: -min(STEPS[i], NZ - STEPS[i]))
FAR_E = sorted(range(1, CHIPS), key=lambda e: -(min(e // NY, NX - e // NY) + min(e % NY, NY - e % NY)))

BIG = 1 << 24
LATE = float(1 << 20)


def unit_rows(embeddings):
    values = embeddings.astype(jnp.float32)
    factor = lax.rsqrt(jnp.mean(values * values, axis=-1, keepdims=True) + 1e-06) * (
        1.0 / math.sqrt(values.shape[-1])
    )
    return (values * factor).astype(jnp.bfloat16)


def iota(shape, axis):
    return lax.broadcasted_iota(jnp.int32, shape, axis)


def one_hot(row, count):
    return jnp.where(iota((count, row.shape[1]), 0) == row, 1.0, 0.0)


def places(member):
    n = member.shape[1]
    before = jnp.where(iota((n, n), 0) < iota((n, n), 1), 1.0, 0.0).astype(jnp.bfloat16)
    counts = jnp.dot(member.astype(jnp.bfloat16), before, preferred_element_type=jnp.float32)
    return jnp.sum(member * counts, axis=0, keepdims=True).astype(jnp.int32)


def three_rows(a, b, c):
    sub = iota((8, a.shape[1]), 0)
    rows = jnp.where(sub == 0, a, jnp.where(sub == 1, b, jnp.where(sub == 2, c, 0.0)))
    return rows.astype(jnp.bfloat16)


def place_codes(codes, hot):
    parts = three_rows(
        (codes >> 16).astype(jnp.float32),
        ((codes >> 8) & 255).astype(jnp.float32),
        (codes & 255).astype(jnp.float32),
    )
    moved = lax.dot_general(parts, hot, (((1,), (1,)), ((), ())), preferred_element_type=jnp.float32)
    return (moved[0:1] * 65536.0 + moved[1:2] * 256.0 + moved[2:3]).astype(jnp.int32)


def fetch_values(values, hot):
    high = values.astype(jnp.bfloat16).astype(jnp.float32)
    rest = values - high
    middle = rest.astype(jnp.bfloat16).astype(jnp.float32)
    parts = three_rows(high, middle, rest - middle)
    moved = jnp.dot(parts, hot, preferred_element_type=jnp.float32)
    return (moved[0:1] + moved[1:2]) + moved[2:3]


def kernel(
    cap,
    emb_in, cluster_in, rank_in, out, flag,
    emb, cluster, rank, hot1, hot2, home, zsend, zrecv, xysend, half_out, half_in, own, other, key_rank,
    zmeta_out, zmeta_in, xymeta_out, xymeta_in, own_meta, other_meta,
    best_out, xyback, zback_out, zback,
    in_sem, zmeta_sem, zrow_send, zrow_recv, xymeta_sem, xyrow_send, xyrow_recv,
    cmeta_sem, crow_send, crow_recv, xyback_sem, zback_sem,
):
    dp, y = lax.axis_index("dp"), lax.axis_index("split")
    x, z, core = dp // (2 * NZ), (dp // 2) % NZ, dp % 2
    lanes = [n * cap for n in COUNTS]
    tiles = [max(1, n // 128) for n in lanes]
    tile0 = [sum(tiles[:g]) for g in range(GROUPS)]

    def along_z(step):
        return ((x * NZ + (z + step + NZ) % NZ) * 2 + core, y)

    def in_plane(e, sign):
        there_x = (x + sign * (e // NY) + NX) % NX
        there_y = (y + sign * (e % NY) + NY) % NY
        return ((there_x * NZ + z) * 2 + core, there_y)

    partner = (dp + 1 - 2 * core, y)

    barrier = pltpu.get_barrier_semaphore()
    for i in FAR_Z:
        pl.semaphore_signal(barrier, inc=1, device_id=along_z(STEPS[i]), device_id_type=MESH)
    for e in FAR_E:
        pl.semaphore_signal(barrier, inc=1, device_id=in_plane(e, 1), device_id_type=MESH)
    pl.semaphore_signal(barrier, inc=1, device_id=partner, device_id_type=MESH)
    loads = [
        pltpu.make_async_copy(src, dst, in_sem.at[n])
        for n, (src, dst) in enumerate(((cluster_in, cluster), (rank_in, rank), (emb_in, emb)))
    ]
    for load in loads:
        load.start()

    def send(src, dst, send_sem, recv_sem, device):
        pltpu.make_async_remote_copy(
            src_ref=src, dst_ref=dst, send_sem=send_sem, recv_sem=recv_sem, device_id=device, device_id_type=MESH
        ).start()

    def wait(ref, sem):
        pltpu.make_async_copy(ref, ref, sem).wait()

    loads[0].wait()
    loads[1].wait()
    ids = cluster[...]
    away = ((ids >> 4) - z) & (NZ - 1)
    step = jnp.zeros_like(ids)
    spot = jnp.zeros_like(ids)
    for i in range(NZ):
        g = GROUP_OF[i]
        step = jnp.where(away == STEPS[i], i, step)
        spot = jnp.where(away == STEPS[i], OFF[g] + MOST * (i - FIRST[g]), spot)
    place = places(one_hot(step, NZ))
    again = places(one_hot(ids, NZ * CHIPS))
    chip = ((((ids >> 2) & 3) - x) & 3) * NY + (((ids & 3) - y) & 3)
    spot = spot + again + chip * jnp.where(step < FIRST[WHOLE], SLOTS[0], SLOTS[WHOLE])
    slot = jnp.where(place < cap, step * cap + place, -1)
    most = jnp.max(place.astype(jnp.float32), axis=1, keepdims=True)
    codes = ((chip * MOST + again) << 17) + rank[...] + 1
    for g in range(GROUPS):
        rows = slice(FIRST[g] * cap, FIRST[g] * cap + lanes[g])
        hot = one_hot(slot - FIRST[g] * cap, lanes[g]).astype(jnp.bfloat16)
        hot1[rows, :] = hot
        placed = jnp.where(most >= cap, BIG, place_codes(codes, hot))
        width = min(128, lanes[g])
        for t in range(tiles[g]):
            zmeta_out[tile0[g] + t, :, 0:width] = placed[:, t * 128 : t * 128 + width]

    def code_row(i):
        g = GROUP_OF[i]
        return zmeta_out.at[tile0[g] + (i - FIRST[g]) * cap // 128]

    zmeta_in[0] = zmeta_out[0]
    loads[2].wait()
    unit = unit_rows(emb[...])
    for g in range(GROUPS):
        at = slice(FIRST[g] * cap, FIRST[g] * cap + lanes[g])
        rows = jnp.dot(hot1[at, :], unit, preferred_element_type=jnp.float32).astype(jnp.bfloat16)
        zsend[at, :] = rows
        if g == 0:
            zrecv[0:cap, :] = rows[0:cap]
            pl.semaphore_wait(barrier, NZ - 1 + CHIPS - 1 + 1)
            for i in FAR_Z:
                send(code_row(i), zmeta_in.at[i], zmeta_sem.at[0], zmeta_sem.at[1], along_z(STEPS[i]))
        for i in range(max(1, FIRST[g]), FIRST[g] + COUNTS[g]):
            span = pl.ds(i * cap, cap)
            send(zsend.at[span], zrecv.at[span], zrow_send.at[0], zrow_recv.at[g], along_z(STEPS[i]))
    home[...] = one_hot(spot, TOTAL).astype(jnp.bfloat16)

    wait(zmeta_in.at[pl.ds(1, NZ - 1)], zmeta_sem.at[1])
    sub8 = iota((8, 128), 0)
    lane8 = iota((8, 128), 1)
    over = jnp.zeros((1, 1), jnp.float32)
    meta = [jnp.zeros((8, 128), jnp.int32), jnp.zeros((8, 128), jnp.int32)]
    for g in range(GROUPS):
        width = min(128, lanes[g])
        parts = []
        for t in range(tiles[g]):
            first = FIRST[g] + t * 128 // cap
            row = zmeta_in[first, :, 0:width]
            for q in range(1, width // cap):
                row = jnp.where(iota((1, width), 1) // cap == q, zmeta_in[first + q, :, 0:width], row)
            parts.append(row)
        codes = parts[0] if tiles[g] == 1 else jnp.concatenate(parts, axis=1)
        over = jnp.maximum(over, jnp.max(codes.astype(jnp.float32), axis=1, keepdims=True))
        filled = (codes > 0) & (codes < BIG)
        value = codes - 1
        source = iota((1, lanes[g]), 1) // cap
        target = (value >> 19) * SLOTS[g] + source * MOST + ((value >> 17) & 3)
        hot = one_hot(jnp.where(filled, target, -1), XG[g]).astype(jnp.bfloat16)
        hot2[OFF[g] : OFF[g] + XG[g], 0 : lanes[g]] = hot
        ranks = place_codes(jnp.where(filled, (value & 131071) + 1, 0), hot)
        for h in range(2):
            part = ranks[:, h * 128 : (h + 1) * 128] if g < WHOLE else ranks
            meta[h] = jnp.where(sub8 == g, part, meta[h])
    for h in range(2):
        xymeta_out[h] = jnp.where(over >= BIG, BIG, meta[h])
    xymeta_in[0] = xymeta_out[0]
    for e in FAR_E:
        send(xymeta_out.at[e // 8], xymeta_in.at[e], xymeta_sem.at[0], xymeta_sem.at[1], in_plane(e, 1))

    def from_chips(ref):
        out = []
        for h in range(2):
            tile = ref[h * 8]
            for e in range(h * 8 + 1, h * 8 + 8):
                owned = ((sub8 < WHOLE) & (lane8 // 16 == e % 8)) | ((sub8 >= WHOLE) & (lane8 // 8 == e))
                tile = jnp.where(owned, ref[e], tile)
            out.append(tile)
        joined = jnp.where(lane8 < 64, out[0], out[1])
        return [jnp.where(sub8 < WHOLE, tile, joined) for tile in out]

    def parts_of(g):
        return 2 if g < WHOLE else 1

    def plane_ranks():
        wait(xymeta_in.at[pl.ds(1, CHIPS - 1)], xymeta_sem.at[1])
        merged = from_chips(xymeta_in)
        for h in range(2):
            own_meta[h] = merged[h]
        send(own_meta, other_meta, cmeta_sem.at[0], cmeta_sem.at[1], partner)

        rows = [[merged[h][g : g + 1].astype(jnp.float32) for h in range(parts_of(g))] for g in range(GROUPS)]
        wait(other_meta, cmeta_sem.at[1])
        top = jnp.zeros((8, 128), jnp.float32)
        for which, ref in enumerate((own_meta, other_meta)):
            for h in range(2):
                tile = ref[h].astype(jnp.float32)
                top = jnp.maximum(top, tile)
                for g in range(GROUPS):
                    if h < parts_of(g):
                        row = tile[g : g + 1]
                        key = jnp.where(row > 0.0, row, LATE)
                        at = which * TOTAL + OFF[g] + h * 128
                        key_rank[at : at + 128, :] = jnp.transpose(jnp.broadcast_to(key, (128, 128)))
        flag[...] = jnp.where(jnp.max(top, axis=(0, 1), keepdims=True) >= BIG, 1, 0)
        return rows

    best = [[jnp.full((1, 128), -1.0, jnp.float32) for _ in range(parts_of(g))] for g in range(GROUPS)]

    def score(which, first, last, g0, g1):
        k0, k1 = OFF[first], OFF[last - 1] + XG[last - 1]
        q0, q1 = OFF[g0], OFF[g1 - 1] + XG[g1 - 1]
        scores = lax.dot_general(
            (own, other)[which][k0:k1, :], own[q0:q1, :], (((1,), (1,)), ((), ())), preferred_element_type=jnp.float32
        )
        ranks = key_rank[which * TOTAL + k0 : which * TOTAL + k1, :]
        for g in range(g0, g1):
            for h in range(parts_of(g)):
                at = OFF[g] - q0 + h * 128
                part = jnp.where(ranks < query_rank[g][h], scores[:, at : at + 128], -1.0)
                best[g][h] = jnp.maximum(best[g][h], jnp.max(part, axis=0, keepdims=True))

    def score_group(which, g):
        score(which, 0, g + 1, g, g + 1)
        if g:
            score(which, g, g + 1, 0, g)

    def group_in_plane(g):
        first, end = max(1, FIRST[g]) * cap, FIRST[g] * cap + lanes[g]
        wait(zrecv.at[pl.ds(first, end - first)], zrow_recv.at[g])
        rows = jnp.dot(
            hot2[OFF[g] : OFF[g] + XG[g], 0 : lanes[g]],
            zrecv[FIRST[g] * cap : end, :],
            preferred_element_type=jnp.float32,
        )
        if g < WHOLE:
            rows = rows.astype(jnp.bfloat16)
            xysend[OFF[g] : OFF[g] + XG[g], :] = rows
            own[OFF[g] : OFF[g] + 16, :] = rows[0:16]
            src, dst, base = xysend, own, OFF[g]
        else:
            rows = rows.reshape(CHIPS, 8, WIDTH)
            rows = jnp.concatenate([rows[:, :, :HALF], rows[:, :, HALF:]], axis=1).reshape(CHIPS * 16, HALF)
            rows = rows.astype(jnp.bfloat16)
            src, dst, base = half_out, half_in, (g - WHOLE) * CHIPS * 16
            half_out[base : base + CHIPS * 16, :] = rows
            half_in[base : base + 16, :] = rows[0:16]
        for e in FAR_E:
            span = pl.ds(base + e * 16, 16)
            send(src.at[span], dst.at[span], xyrow_send.at[g], xyrow_recv.at[g], in_plane(e, 1))

    def wait_plane(g, sem):
        ref, base = (own, OFF[g]) if g < WHOLE else (half_in, (g - WHOLE) * CHIPS * 16)
        wait(ref.at[pl.ds(base + 16, CHIPS * 16 - 16)], sem)

    def group_to_partner(g):
        wait_plane(g, xyrow_recv.at[g])
        if g >= WHOLE:
            base = (g - WHOLE) * CHIPS * 16
            rows = half_in[base : base + CHIPS * 16, :].astype(jnp.float32).reshape(CHIPS, 16, HALF)
            rows = jnp.concatenate([rows[:, :8], rows[:, 8:]], axis=2).reshape(CHIPS * 8, WIDTH)
            own[OFF[g] : OFF[g] + XG[g], :] = rows.astype(jnp.bfloat16)
        span = pl.ds(OFF[g], XG[g])
        send(own.at[span], other.at[span], crow_send.at[0], crow_recv.at[g], partner)

    def group_from_partner(g):
        wait(other.at[pl.ds(OFF[g], XG[g])], crow_recv.at[g])

    for g in range(GROUPS):
        group_in_plane(g)
        if g == 0:
            query_rank = plane_ranks()
        if g >= 1:
            group_to_partner(g - 1)
        if g >= 2:
            group_from_partner(g - 2)
            for which in range(2):
                score_group(which, g - 2)
    group_from_partner(GROUPS - 2)
    for which in range(2):
        score_group(which, GROUPS - 2)
    group_to_partner(GROUPS - 1)
    score_group(0, GROUPS - 1)
    group_from_partner(GROUPS - 1)
    score_group(1, GROUPS - 1)

    for h in range(2):
        tile = jnp.zeros((8, 128), jnp.float32)
        for g in range(GROUPS):
            tile = jnp.where(sub8 == g, best[g][h if g < WHOLE else 0], tile)
        best_out[h] = tile
    xyback[0] = best_out[0]
    for e in FAR_E:
        send(best_out.at[e // 8], xyback.at[e], xyback_sem.at[0], xyback_sem.at[1], in_plane(e, -1))
    wait(xyback.at[pl.ds(1, CHIPS - 1)], xyback_sem.at[1])
    merged = from_chips(xyback)
    for g in range(GROUPS):
        for h in range(2):
            zback_out[g, h : h + 1, :] = merged[h][g : g + 1]
    zback[0] = zback_out[0]
    for i in FAR_Z:
        send(zback_out.at[GROUP_OF[i]], zback.at[i], zback_sem.at[0], zback_sem.at[1], along_z(-STEPS[i]))
    wait(zback.at[pl.ds(1, NZ - 1)], zback_sem.at[1])
    parts = []
    lane2 = iota((2, 128), 1)
    for g in range(GROUPS):
        row = zback[FIRST[g]]
        for q in range(1, COUNTS[g]):
            row = jnp.where((lane2 // MOST) % COUNTS[g] == q, zback[FIRST[g] + q], row)
        parts += [row[h : h + 1] for h in range(parts_of(g))]
    out[...] = fetch_values(jnp.concatenate(parts, axis=1), home[...])

    wait(zmeta_in.at[pl.ds(1, NZ - 1)], zmeta_sem.at[0])
    wait(zsend.at[pl.ds(cap, (NZ - 1) * cap)], zrow_send.at[0])
    wait(xymeta_in.at[pl.ds(1, CHIPS - 1)], xymeta_sem.at[0])
    for g in range(GROUPS):
        wait_plane(g, xyrow_send.at[g])
    wait(own_meta, cmeta_sem.at[0])
    wait(own, crow_send.at[0])
    wait(xyback.at[pl.ds(1, CHIPS - 1)], xyback_sem.at[0])
    wait(zback.at[pl.ds(1, NZ - 1)], zback_sem.at[0])


def exchange(cap, collective_id, embeddings, cluster_ids, order_ranks):
    vmem = pl.BlockSpec(memory_space=pltpu.VMEM)
    anywhere = pl.BlockSpec(memory_space=pl.ANY)
    bf16, f32, i32 = jnp.bfloat16, jnp.float32, jnp.int32
    rows_of_codes = sum(max(1, n * cap // 128) for n in COUNTS)

    def sems(n):
        return pltpu.SemaphoreType.DMA((n,))

    return pl.pallas_call(
        partial(kernel, cap),
        out_shape=(jax.ShapeDtypeStruct((1, ROWS), f32), jax.ShapeDtypeStruct((1, 1), i32)),
        in_specs=[anywhere] * 3,
        out_specs=(vmem, vmem),
        scratch_shapes=[
            pltpu.VMEM((ROWS, WIDTH), bf16),
            pltpu.VMEM((1, ROWS), i32),
            pltpu.VMEM((1, ROWS), i32),
            pltpu.VMEM((NZ * cap, ROWS), bf16),
            pltpu.VMEM((TOTAL, MOST * cap), bf16),
            pltpu.VMEM((TOTAL, ROWS), bf16),
            pltpu.VMEM((NZ * cap, WIDTH), bf16),
            pltpu.VMEM((NZ * cap, WIDTH), bf16),
            pltpu.VMEM((OFF[WHOLE], WIDTH), bf16),
            pltpu.VMEM(((GROUPS - WHOLE) * CHIPS * 16, HALF), bf16),
            pltpu.VMEM(((GROUPS - WHOLE) * CHIPS * 16, HALF), bf16),
            pltpu.VMEM((TOTAL, WIDTH), bf16),
            pltpu.VMEM((TOTAL, WIDTH), bf16),
            pltpu.VMEM((2 * TOTAL, 128), f32),
            pltpu.VMEM((rows_of_codes, 1, 128), i32),
            pltpu.VMEM((NZ, 1, 128), i32),
            pltpu.VMEM((2, 8, 128), i32),
            pltpu.VMEM((CHIPS, 8, 128), i32),
            pltpu.VMEM((2, 8, 128), i32),
            pltpu.VMEM((2, 8, 128), i32),
            pltpu.VMEM((2, 8, 128), f32),
            pltpu.VMEM((CHIPS, 8, 128), f32),
            pltpu.VMEM((GROUPS, 2, 128), f32),
            pltpu.VMEM((NZ, 2, 128), f32),
            sems(3), sems(2), sems(1), sems(GROUPS), sems(2), sems(GROUPS), sems(GROUPS),
            sems(2), sems(1), sems(GROUPS), sems(2), sems(2),
        ],
        compiler_params=pltpu.CompilerParams(
            collective_id=collective_id, has_side_effects=True, vmem_limit_bytes=40 * 1024 * 1024
        ),
    )(embeddings, cluster_ids, order_ranks)


def shards(embeddings, cluster_ids, order_ranks):
    args = (embeddings, cluster_ids.reshape(1, ROWS), order_ranks.reshape(1, ROWS))
    nearest, flag = exchange(CAP, 0, *args)
    nearest = lax.cond(flag[0, 0] > 0, lambda: exchange(FULL, 1, *args)[0], lambda: nearest)
    return nearest.reshape(ROWS)


def solution(mesh):
    in_specs = (P(("dp", "split"), None), P(("dp", "split"), None), P(("dp", "split")))
    out_specs = P(("dp", "split"))
    return jax.shard_map(shards, mesh=mesh, in_specs=in_specs, out_specs=out_specs, check_vma=False)
```

```python
from functools import partial
import math

import jax
import jax.numpy as jnp
from jax import lax
from jax.experimental import pallas as pl
from jax.experimental.pallas import tpu as pltpu
from jax.sharding import PartitionSpec as P

MESH = pl.DeviceIdType.MESH

NX, NY, NZ = 4, 4, 16
CHIPS = NX * NY
ROWS = 256
WIDTH = 768
HALF = WIDTH // 2
MOST = 4
CAP = 32
FULL = MOST * CHIPS

STEPS = [0, 8, 4, 12, 7, 9, 1, 15, 6, 10, 2, 14, 3, 13, 5, 11]
COUNTS = [4, 4, 4, 2, 2]
GROUPS = len(COUNTS)
FIRST = [sum(COUNTS[:g]) for g in range(GROUPS)]
GROUP_OF = [g for g in range(GROUPS) for _ in range(COUNTS[g])]
SLOTS = [MOST * n for n in COUNTS]
XG = [CHIPS * n for n in SLOTS]
OFF = [sum(XG[:g]) for g in range(GROUPS)]
TOTAL = sum(XG)
WHOLE = 3
FAR_Z = sorted(range(1, NZ), key=lambda i: -min(STEPS[i], NZ - STEPS[i]))
FAR_E = sorted(range(1, CHIPS), key=lambda e: -(min(e // NY, NX - e // NY) + min(e % NY, NY - e % NY)))

RELAY = NZ // 4
NEAR_Z = [i for i in FAR_Z if min(STEPS[i], NZ - STEPS[i]) <= RELAY]
BEYOND_Z = [i for i in FAR_Z if i not in NEAR_Z]
SEND_NEAR = [4, 12]
SEND = [8, 7, 9, 1, 15, 6, 10, 2, 14, 3, 13, 5, 11]

BIG = 1 << 24
LATE = float(1 << 20)


def unit_rows(embeddings):
    values = embeddings.astype(jnp.float32)
    factor = lax.rsqrt(jnp.mean(values * values, axis=-1, keepdims=True) + 1e-06) * (
        1.0 / math.sqrt(values.shape[-1])
    )
    return (values * factor).astype(jnp.bfloat16)


def iota(shape, axis):
    return lax.broadcasted_iota(jnp.int32, shape, axis)


def one_hot(row, count):
    return jnp.where(iota((count, row.shape[1]), 0) == row, 1.0, 0.0)


def places(member):
    n = member.shape[1]
    before = jnp.where(iota((n, n), 0) < iota((n, n), 1), 1.0, 0.0).astype(jnp.bfloat16)
    counts = jnp.dot(member.astype(jnp.bfloat16), before, preferred_element_type=jnp.float32)
    return jnp.sum(member * counts, axis=0, keepdims=True).astype(jnp.int32)


def three_rows(a, b, c):
    sub = iota((8, a.shape[1]), 0)
    rows = jnp.where(sub == 0, a, jnp.where(sub == 1, b, jnp.where(sub == 2, c, 0.0)))
    return rows.astype(jnp.bfloat16)


def place_codes(codes, hot):
    parts = three_rows(
        (codes >> 16).astype(jnp.float32),
        ((codes >> 8) & 255).astype(jnp.float32),
        (codes & 255).astype(jnp.float32),
    )
    moved = lax.dot_general(parts, hot, (((1,), (1,)), ((), ())), preferred_element_type=jnp.float32)
    return (moved[0:1] * 65536.0 + moved[1:2] * 256.0 + moved[2:3]).astype(jnp.int32)


def fetch_values(values, hot):
    high = values.astype(jnp.bfloat16).astype(jnp.float32)
    rest = values - high
    middle = rest.astype(jnp.bfloat16).astype(jnp.float32)
    parts = three_rows(high, middle, rest - middle)
    moved = jnp.dot(parts, hot, preferred_element_type=jnp.float32)
    return (moved[0:1] + moved[1:2]) + moved[2:3]


def kernel(
    cap,
    emb_in, cluster_in, rank_in, out, flag,
    emb, cluster, rank, hot1, hot2, home, zsend, zrecv, xysend, half_out, half_in, half_other, own, other, key_rank,
    zmeta_out, zmeta_in, xymeta_out, xymeta_in, own_meta, other_meta,
    best_out, xyback, zback_out, zback,
    beyond, in_sem, zmeta_sem, zrow_send, zrow_recv, xymeta_sem, xyrow_send, xyrow_recv,
    cmeta_sem, crow_send, crow_recv, xyback_sem, zback_sem,
):
    dp, y = lax.axis_index("dp"), lax.axis_index("split")
    x, z, core = dp // (2 * NZ), (dp // 2) % NZ, dp % 2
    lanes = [n * cap for n in COUNTS]
    tiles = [max(1, n // 128) for n in lanes]
    tile0 = [sum(tiles[:g]) for g in range(GROUPS)]

    def along_z(step):
        return ((x * NZ + (z + step + NZ) % NZ) * 2 + core, y)

    def in_plane(e, sign):
        there_x = (x + sign * (e // NY) + NX) % NX
        there_y = (y + sign * (e % NY) + NY) % NY
        return ((there_x * NZ + z) * 2 + core, there_y)

    partner = (dp + 1 - 2 * core, y)

    barrier = pltpu.get_barrier_semaphore()
    for i in NEAR_Z:
        pl.semaphore_signal(barrier, inc=1, device_id=along_z(STEPS[i]), device_id_type=MESH)
    for e in FAR_E:
        pl.semaphore_signal(barrier, inc=1, device_id=in_plane(e, 1), device_id_type=MESH)
    pl.semaphore_signal(barrier, inc=1, device_id=partner, device_id_type=MESH)
    loads = [
        pltpu.make_async_copy(src, dst, in_sem.at[n])
        for n, (src, dst) in enumerate(((cluster_in, cluster), (rank_in, rank), (emb_in, emb)))
    ]
    for load in loads:
        load.start()

    def send(src, dst, send_sem, recv_sem, device):
        pltpu.make_async_remote_copy(
            src_ref=src, dst_ref=dst, send_sem=send_sem, recv_sem=recv_sem, device_id=device, device_id_type=MESH
        ).start()

    def wait(ref, sem):
        pltpu.make_async_copy(ref, ref, sem).wait()

    loads[0].wait()
    loads[1].wait()
    ids = cluster[...]
    away = ((ids >> 4) - z) & (NZ - 1)
    step = jnp.zeros_like(ids)
    spot = jnp.zeros_like(ids)
    for i in range(NZ):
        g = GROUP_OF[i]
        step = jnp.where(away == STEPS[i], i, step)
        spot = jnp.where(away == STEPS[i], OFF[g] + MOST * (i - FIRST[g]), spot)
    place = places(one_hot(step, NZ))
    again = places(one_hot(ids, NZ * CHIPS))
    chip = ((((ids >> 2) & 3) - x) & 3) * NY + (((ids & 3) - y) & 3)
    spot = spot + again + chip * jnp.where(step < FIRST[WHOLE], SLOTS[0], SLOTS[WHOLE])
    slot = jnp.where(place < cap, step * cap + place, -1)
    most = jnp.max(place.astype(jnp.float32), axis=1, keepdims=True)
    codes = ((chip * MOST + again) << 17) + rank[...] + 1
    for g in range(GROUPS):
        rows = slice(FIRST[g] * cap, FIRST[g] * cap + lanes[g])
        hot = one_hot(slot - FIRST[g] * cap, lanes[g]).astype(jnp.bfloat16)
        hot1[rows, :] = hot
        placed = jnp.where(most >= cap, BIG, place_codes(codes, hot))
        width = min(128, lanes[g])
        for t in range(tiles[g]):
            zmeta_out[tile0[g] + t, :, 0:width] = placed[:, t * 128 : t * 128 + width]

    def code_row(i):
        g = GROUP_OF[i]
        return zmeta_out.at[tile0[g] + (i - FIRST[g]) * cap // 128]

    zmeta_in[0] = zmeta_out[0]
    loads[2].wait()
    unit = unit_rows(emb[...])
    for g in range(GROUPS):
        at = slice(FIRST[g] * cap, FIRST[g] * cap + lanes[g])
        rows = jnp.dot(hot1[at, :], unit, preferred_element_type=jnp.float32).astype(jnp.bfloat16)
        zsend[at, :] = rows
        if g == 0:
            zrecv[0:cap, :] = rows[0:cap]

    def send_rows(i):
        span = pl.ds(i * cap, cap)
        send(zsend.at[span], zrecv.at[span], zrow_send.at[0], zrow_recv.at[GROUP_OF[i]], along_z(STEPS[i]))

    def send_codes(i):
        send(code_row(i), zmeta_in.at[i], zmeta_sem.at[0], zmeta_sem.at[1], along_z(STEPS[i]))

    pl.semaphore_wait(barrier, len(NEAR_Z) + CHIPS - 1 + 1)
    for to in (RELAY, -RELAY):
        pl.semaphore_signal(beyond, inc=1, device_id=along_z(to), device_id_type=MESH)
    for i in NEAR_Z:
        send_codes(i)
    for d in SEND_NEAR:
        send_rows(STEPS.index(d))
    pl.semaphore_wait(beyond, 2)
    for i in BEYOND_Z:
        send_codes(i)
    for d in SEND:
        send_rows(STEPS.index(d))
    home[...] = one_hot(spot, TOTAL).astype(jnp.bfloat16)

    wait(zmeta_in.at[pl.ds(1, NZ - 1)], zmeta_sem.at[1])
    sub8 = iota((8, 128), 0)
    lane8 = iota((8, 128), 1)
    over = jnp.zeros((1, 1), jnp.float32)
    meta = [jnp.zeros((8, 128), jnp.int32), jnp.zeros((8, 128), jnp.int32)]
    for g in range(GROUPS):
        width = min(128, lanes[g])
        parts = []
        for t in range(tiles[g]):
            first = FIRST[g] + t * 128 // cap
            row = zmeta_in[first, :, 0:width]
            for q in range(1, width // cap):
                row = jnp.where(iota((1, width), 1) // cap == q, zmeta_in[first + q, :, 0:width], row)
            parts.append(row)
        codes = parts[0] if tiles[g] == 1 else jnp.concatenate(parts, axis=1)
        over = jnp.maximum(over, jnp.max(codes.astype(jnp.float32), axis=1, keepdims=True))
        filled = (codes > 0) & (codes < BIG)
        value = codes - 1
        source = iota((1, lanes[g]), 1) // cap
        target = (value >> 19) * SLOTS[g] + source * MOST + ((value >> 17) & 3)
        hot = one_hot(jnp.where(filled, target, -1), XG[g]).astype(jnp.bfloat16)
        hot2[OFF[g] : OFF[g] + XG[g], 0 : lanes[g]] = hot
        ranks = place_codes(jnp.where(filled, (value & 131071) + 1, 0), hot)
        for h in range(2):
            part = ranks[:, h * 128 : (h + 1) * 128] if g < WHOLE else ranks
            meta[h] = jnp.where(sub8 == g, part, meta[h])
    for h in range(2):
        xymeta_out[h] = jnp.where(over >= BIG, BIG, meta[h])
    xymeta_in[0] = xymeta_out[0]
    for e in FAR_E:
        send(xymeta_out.at[e // 8], xymeta_in.at[e], xymeta_sem.at[0], xymeta_sem.at[1], in_plane(e, 1))

    def from_chips(ref):
        out = []
        for h in range(2):
            tile = ref[h * 8]
            for e in range(h * 8 + 1, h * 8 + 8):
                owned = ((sub8 < WHOLE) & (lane8 // 16 == e % 8)) | ((sub8 >= WHOLE) & (lane8 // 8 == e))
                tile = jnp.where(owned, ref[e], tile)
            out.append(tile)
        joined = jnp.where(lane8 < 64, out[0], out[1])
        return [jnp.where(sub8 < WHOLE, tile, joined) for tile in out]

    def parts_of(g):
        return 2 if g < WHOLE else 1

    def plane_ranks():
        wait(xymeta_in.at[pl.ds(1, CHIPS - 1)], xymeta_sem.at[1])
        merged = from_chips(xymeta_in)
        for h in range(2):
            own_meta[h] = merged[h]
        send(own_meta, other_meta, cmeta_sem.at[0], cmeta_sem.at[1], partner)

        rows = [[merged[h][g : g + 1].astype(jnp.float32) for h in range(parts_of(g))] for g in range(GROUPS)]
        wait(other_meta, cmeta_sem.at[1])
        top = jnp.zeros((8, 128), jnp.float32)
        for which, ref in enumerate((own_meta, other_meta)):
            for h in range(2):
                tile = ref[h].astype(jnp.float32)
                top = jnp.maximum(top, tile)
                for g in range(GROUPS):
                    if h < parts_of(g):
                        row = tile[g : g + 1]
                        key = jnp.where(row > 0.0, row, LATE)
                        at = which * TOTAL + OFF[g] + h * 128
                        key_rank[at : at + 128, :] = jnp.transpose(jnp.broadcast_to(key, (128, 128)))
        flag[...] = jnp.where(jnp.max(top, axis=(0, 1), keepdims=True) >= BIG, 1, 0)
        return rows

    best = [[jnp.full((1, 128), -1.0, jnp.float32) for _ in range(parts_of(g))] for g in range(GROUPS)]

    def score(which, first, last, g0, g1):
        k0, k1 = OFF[first], OFF[last - 1] + XG[last - 1]
        q0, q1 = OFF[g0], OFF[g1 - 1] + XG[g1 - 1]
        scores = lax.dot_general(
            (own, other)[which][k0:k1, :], own[q0:q1, :], (((1,), (1,)), ((), ())), preferred_element_type=jnp.float32
        )
        ranks = key_rank[which * TOTAL + k0 : which * TOTAL + k1, :]
        for g in range(g0, g1):
            for h in range(parts_of(g)):
                at = OFF[g] - q0 + h * 128
                part = jnp.where(ranks < query_rank[g][h], scores[:, at : at + 128], -1.0)
                best[g][h] = jnp.maximum(best[g][h], jnp.max(part, axis=0, keepdims=True))

    def score_own(g):
        score(0, 0, g + 1, g, g + 1)
        if g:
            score(1, 0, g, g, g + 1)
            score(0, g, g + 1, 0, g)

    def score_other(g):
        score(1, g, g + 1, 0, g + 1)

    def group_in_plane(g):
        first, end = max(1, FIRST[g]) * cap, FIRST[g] * cap + lanes[g]
        wait(zrecv.at[pl.ds(first, end - first)], zrow_recv.at[g])
        rows = jnp.dot(
            hot2[OFF[g] : OFF[g] + XG[g], 0 : lanes[g]],
            zrecv[FIRST[g] * cap : end, :],
            preferred_element_type=jnp.float32,
        )
        if g < WHOLE:
            rows = rows.astype(jnp.bfloat16)
            xysend[OFF[g] : OFF[g] + XG[g], :] = rows
            own[OFF[g] : OFF[g] + 16, :] = rows[0:16]
            src, dst, base = xysend, own, OFF[g]
        else:
            rows = rows.reshape(CHIPS, 8, WIDTH)
            rows = jnp.concatenate([rows[:, :, :HALF], rows[:, :, HALF:]], axis=1).reshape(CHIPS * 16, HALF)
            rows = rows.astype(jnp.bfloat16)
            src, dst, base = half_out, half_in, (g - WHOLE) * CHIPS * 16
            half_out[base : base + CHIPS * 16, :] = rows
            half_in[base : base + 16, :] = rows[0:16]
        for e in FAR_E:
            span = pl.ds(base + e * 16, 16)
            send(src.at[span], dst.at[span], xyrow_send.at[g], xyrow_recv.at[g], in_plane(e, 1))

    def wait_plane(g, sem):
        ref, base = (own, OFF[g]) if g < WHOLE else (half_in, (g - WHOLE) * CHIPS * 16)
        wait(ref.at[pl.ds(base + 16, CHIPS * 16 - 16)], sem)

    def to_partner(g):
        if g < WHOLE:
            return own, other, pl.ds(OFF[g], XG[g])
        return half_in, half_other, pl.ds((g - WHOLE) * CHIPS * 16, CHIPS * 16)

    def full_width(ref, g):
        base = (g - WHOLE) * CHIPS * 16
        rows = ref[base : base + CHIPS * 16, :].astype(jnp.float32).reshape(CHIPS, 16, HALF)
        rows = jnp.concatenate([rows[:, :8], rows[:, 8:]], axis=2).reshape(CHIPS * 8, WIDTH)
        return rows.astype(jnp.bfloat16)

    def group_to_partner(g):
        wait_plane(g, xyrow_recv.at[g])
        src, dst, span = to_partner(g)
        send(src.at[span], dst.at[span], crow_send.at[g], crow_recv.at[g], partner)
        if g >= WHOLE:
            own[OFF[g] : OFF[g] + XG[g], :] = full_width(half_in, g)

    def group_from_partner(g):
        _, dst, span = to_partner(g)
        wait(dst.at[span], crow_recv.at[g])
        if g >= WHOLE:
            other[OFF[g] : OFF[g] + XG[g], :] = full_width(half_other, g)

    for g in range(GROUPS):
        group_in_plane(g)
        if g == 0:
            query_rank = plane_ranks()
        if g >= 1:
            group_to_partner(g - 1)
        if g >= 2:
            score_own(g - 2)
            group_from_partner(g - 2)
            score_other(g - 2)
    score_own(GROUPS - 2)
    group_from_partner(GROUPS - 2)
    score_other(GROUPS - 2)
    group_to_partner(GROUPS - 1)
    score_own(GROUPS - 1)
    group_from_partner(GROUPS - 1)
    score_other(GROUPS - 1)

    for h in range(2):
        tile = jnp.zeros((8, 128), jnp.float32)
        for g in range(GROUPS):
            tile = jnp.where(sub8 == g, best[g][h if g < WHOLE else 0], tile)
        best_out[h] = tile
    xyback[0] = best_out[0]
    for e in FAR_E:
        send(best_out.at[e // 8], xyback.at[e], xyback_sem.at[0], xyback_sem.at[1], in_plane(e, -1))
    wait(xyback.at[pl.ds(1, CHIPS - 1)], xyback_sem.at[1])
    merged = from_chips(xyback)
    for g in range(GROUPS):
        for h in range(2):
            zback_out[g, h : h + 1, :] = merged[h][g : g + 1]
    zback[0] = zback_out[0]
    for i in FAR_Z:
        send(zback_out.at[GROUP_OF[i]], zback.at[i], zback_sem.at[0], zback_sem.at[1], along_z(-STEPS[i]))
    wait(zback.at[pl.ds(1, NZ - 1)], zback_sem.at[1])
    parts = []
    lane2 = iota((2, 128), 1)
    for g in range(GROUPS):
        row = zback[FIRST[g]]
        for q in range(1, COUNTS[g]):
            row = jnp.where((lane2 // MOST) % COUNTS[g] == q, zback[FIRST[g] + q], row)
        parts += [row[h : h + 1] for h in range(parts_of(g))]
    out[...] = fetch_values(jnp.concatenate(parts, axis=1), home[...])

    wait(zmeta_in.at[pl.ds(1, NZ - 1)], zmeta_sem.at[0])
    wait(zsend.at[pl.ds(cap, (NZ - 1) * cap)], zrow_send.at[0])
    wait(xymeta_in.at[pl.ds(1, CHIPS - 1)], xymeta_sem.at[0])
    for g in range(GROUPS):
        wait_plane(g, xyrow_send.at[g])
    wait(own_meta, cmeta_sem.at[0])
    for g in range(GROUPS):
        _, dst, span = to_partner(g)
        wait(dst.at[span], crow_send.at[g])
    wait(xyback.at[pl.ds(1, CHIPS - 1)], xyback_sem.at[0])
    wait(zback.at[pl.ds(1, NZ - 1)], zback_sem.at[0])


def exchange(cap, collective_id, embeddings, cluster_ids, order_ranks):
    vmem = pl.BlockSpec(memory_space=pltpu.VMEM)
    anywhere = pl.BlockSpec(memory_space=pl.ANY)
    bf16, f32, i32 = jnp.bfloat16, jnp.float32, jnp.int32
    rows_of_codes = sum(max(1, n * cap // 128) for n in COUNTS)

    def sems(n):
        return pltpu.SemaphoreType.DMA((n,))

    return pl.pallas_call(
        partial(kernel, cap),
        out_shape=(jax.ShapeDtypeStruct((1, ROWS), f32), jax.ShapeDtypeStruct((1, 1), i32)),
        in_specs=[anywhere] * 3,
        out_specs=(vmem, vmem),
        scratch_shapes=[
            pltpu.VMEM((ROWS, WIDTH), bf16),
            pltpu.VMEM((1, ROWS), i32),
            pltpu.VMEM((1, ROWS), i32),
            pltpu.VMEM((NZ * cap, ROWS), bf16),
            pltpu.VMEM((TOTAL, MOST * cap), bf16),
            pltpu.VMEM((TOTAL, ROWS), bf16),
            pltpu.VMEM((NZ * cap, WIDTH), bf16),
            pltpu.VMEM((NZ * cap, WIDTH), bf16),
            pltpu.VMEM((OFF[WHOLE], WIDTH), bf16),
            pltpu.VMEM(((GROUPS - WHOLE) * CHIPS * 16, HALF), bf16),
            pltpu.VMEM(((GROUPS - WHOLE) * CHIPS * 16, HALF), bf16),
            pltpu.VMEM(((GROUPS - WHOLE) * CHIPS * 16, HALF), bf16),
            pltpu.VMEM((TOTAL, WIDTH), bf16),
            pltpu.VMEM((TOTAL, WIDTH), bf16),
            pltpu.VMEM((2 * TOTAL, 128), f32),
            pltpu.VMEM((rows_of_codes, 1, 128), i32),
            pltpu.VMEM((NZ, 1, 128), i32),
            pltpu.VMEM((2, 8, 128), i32),
            pltpu.VMEM((CHIPS, 8, 128), i32),
            pltpu.VMEM((2, 8, 128), i32),
            pltpu.VMEM((2, 8, 128), i32),
            pltpu.VMEM((2, 8, 128), f32),
            pltpu.VMEM((CHIPS, 8, 128), f32),
            pltpu.VMEM((GROUPS, 2, 128), f32),
            pltpu.VMEM((NZ, 2, 128), f32),
            pltpu.SemaphoreType.REGULAR, sems(3), sems(2), sems(1), sems(GROUPS), sems(2), sems(GROUPS), sems(GROUPS),
            sems(2), sems(GROUPS), sems(GROUPS), sems(2), sems(2),
        ],
        compiler_params=pltpu.CompilerParams(
            collective_id=collective_id, has_side_effects=True, vmem_limit_bytes=60 * 1024 * 1024
        ),
    )(embeddings, cluster_ids, order_ranks)


def shards(embeddings, cluster_ids, order_ranks):
    args = (embeddings, cluster_ids.reshape(1, ROWS), order_ranks.reshape(1, ROWS))
    nearest, flag = exchange(CAP, 0, *args)
    nearest = lax.cond(flag[0, 0] > 0, lambda: exchange(FULL, 1, *args)[0], lambda: nearest)
    return nearest.reshape(ROWS)


def solution(mesh):
    in_specs = (P(("dp", "split"), None), P(("dp", "split"), None), P(("dp", "split")))
    out_specs = P(("dp", "split"))
    return jax.shard_map(shards, mesh=mesh, in_specs=in_specs, out_specs=out_specs, check_vma=False)
```
